32 devices in a mesh: groups: 2 (over y), dp: 16 (over z, x, core).
Axes of the slice: x: 2, y: 2, z: 4, core: 2. Of those that a mesh axis runs over, the one named last changes fastest.
Arguments:
- hidden_in: bfloat16 [2, 4096, 14336], P(None, ('groups', 'dp')), parts along dimension 1, may hold values from -6 to 6
- out_grad: bfloat16 [2, 4096, 4096], P(None, ('groups', 'dp')), parts along dimension 1, may hold values from -6 to 6
- proj_hidden: bfloat16 [2, 14336, 64], P(None, 'dp'), may hold values from -0.046875 to 0.046875
- proj_out: bfloat16 [2, 4096, 64], replicated, may hold values from -0.09375 to 0.09375
- lengths: int32 [32], P(('groups', 'dp')), parts along dimension 0, may hold values from 64 to 128
- query_sketch: bfloat16 [512, 8192], P(('groups', 'dp')), parts along dimension 0, may hold values from -6 to 6
Outputs:
- scores: float32 [512, 16], P(('groups', 'dp')), parts along dimension 0
The draws below stay inside these ranges and needn't reach their ends.
There are 2 independent parts, one for each index of `groups`. The reference program is written for one: setup_inputs(seed, part) draws one part's arguments, and reference() takes and returns one part's arrays. A program takes and returns all parts, laid end to end along the dimension named above; an argument that names none is the same for every part. Nothing has to cross between parts.
All inputs are finite; a program needn't handle non-finite values.
Results may differ from the reference program's by a relative error of at most 0.0029.
Values may be sent and summed in bfloat16 or wider, within the bound.
A program may use at most 64 MiB of HBM per device.

```python
import math
import jax
import jax.numpy as jnp
from jax import lax

D = 4096
HID = 14336
R = 64
LAYERS = 2
LEN = 128
EXAMPLES = 16
TOKENS = 2048
QUERIES = 256


def plant(array, rng, low, largest):
    longest = array.shape.index(max(array.shape))
    spots = []
    for shift in (0, 1):
        where = [jax.random.randint(jax.random.fold_in(rng, axis), (), 0, length) for axis, length in enumerate(array.shape)]
        where[longest] = (where[longest] + shift) % array.shape[longest]
        spots.append(tuple(where))
    return array.at[spots[0]].set(low).at[spots[1]].set(largest)


def block_scale(stream_key, extent, cuts, low, top_value):
    level = 1.0
    for dim, parts in cuts:
        draws = jax.random.uniform(jax.random.fold_in(jax.random.fold_in(stream_key, 6), dim), (parts,), jnp.float32, low / len(cuts), top_value / len(cuts))
        level = level * jnp.repeat(jnp.exp(draws), extent[dim] // parts).reshape((-1,) + (1,) * (len(extent) - 1 - dim))
    return level


def centred(stream_key, extent, deviation, most, shards=(), held_as=jnp.bfloat16):
    array = jax.random.normal(stream_key, extent, jnp.float32) * deviation
    if len(shards) > 0:
        array = block_scale(stream_key, extent, shards, -0.22, 0.18) * array
    return jnp.clip(array, min=-most, max=most).astype(held_as)


def setup_inputs(seed: int = 0, part: int = 0) -> dict:
    splits = jax.random.split(jax.random.key(seed), 7)
    part_splits = jax.random.split(jax.random.fold_in(splits[6], part), 7)
    hidden_in = centred(part_splits[0], (LAYERS, TOKENS, HID), 1.0, 6.0, ((1, 16),))
    out_grad = centred(part_splits[1], (LAYERS, TOKENS, D), 1.0, 6.0, ((1, 16),))
    proj_hidden = centred(splits[2], (LAYERS, HID, R), HID ** -0.5, 0.046875, ((1, 16),))
    proj_out = centred(splits[3], (LAYERS, D, R), D ** -0.5, 0.09375)
    lengths = plant(jax.random.randint(part_splits[4], (EXAMPLES,), LEN // 2, LEN + 1), jax.random.fold_in(part_splits[4], 1), LEN // 2, LEN).astype(jnp.int32)
    query_sketch = centred(part_splits[5], (QUERIES, LAYERS * R * R), 1.0, 6.0, ((0, 16),))
    return dict(hidden_in=hidden_in, out_grad=out_grad, proj_hidden=proj_hidden, proj_out=proj_out, lengths=lengths, query_sketch=query_sketch)


def reference(hidden_in, out_grad, proj_hidden, proj_out, lengths, query_sketch):
    position = jnp.arange(TOKENS, dtype=jnp.int32)
    length_limit = jnp.repeat(lengths, LEN)
    kept_mask = (position % LEN < length_limit).astype(jnp.float32)
    sketches = []
    for layer in range(LAYERS):
        projected_in = jnp.dot(hidden_in[layer], proj_hidden[layer], preferred_element_type=jnp.float32)
        projected_out = jnp.dot(out_grad[layer], proj_out[layer], preferred_element_type=jnp.float32)
        projected_out = projected_out * kept_mask[:, None]
        sketch = jnp.einsum('epa,epb->eab', projected_out.reshape(EXAMPLES, LEN, R), projected_in.reshape(EXAMPLES, LEN, R), precision=lax.Precision.HIGHEST)
        sketches.append(sketch * (1.0 / math.sqrt(LEN)))
    stacked = jnp.stack(sketches, axis=1).reshape(EXAMPLES, LAYERS * R * R).astype(jnp.bfloat16)
    product = jnp.dot(query_sketch, stacked.T, preferred_element_type=jnp.float32)
    return product * (1.0 / math.sqrt(LAYERS * R * R))
```

```python
import functools
import math

import jax
import jax.numpy as jnp
from jax import lax
from jax.experimental import pallas as pl
from jax.experimental.pallas import tpu as pltpu
from jax.sharding import PartitionSpec as P

LEN = 128
MESH = pl.DeviceIdType.MESH
ROWS_BY_ROWS = (((1,), (1,)), ((), ()))


def plain(hidden_in, out_grad, proj_hidden, proj_out, lengths, query_sketch):
    layer_count = hidden_in.shape[0]
    rank_size = proj_out.shape[2]
    tok_rows = out_grad.shape[1]
    seq_count = lengths.shape[0]
    position = jnp.arange(tok_rows, dtype=jnp.int32)
    length_limit = jnp.repeat(lengths, LEN)
    kept_mask = (position % LEN < length_limit).astype(jnp.float32)
    inputs = jnp.einsum(
        "lth,lhr->ltr",
        hidden_in,
        lax.all_gather(proj_hidden, "dp", axis=1, tiled=True),
        preferred_element_type=jnp.float32,
    )
    sketches = []
    for layer in range(layer_count):
        projected_out = jnp.dot(
            out_grad[layer], proj_out[layer], preferred_element_type=jnp.float32
        )
        projected_out = projected_out * kept_mask[:, None]
        sketch = jnp.einsum(
            "epa,epb->eab",
            projected_out.reshape(seq_count, LEN, rank_size),
            inputs[layer].reshape(seq_count, LEN, rank_size),
            precision=lax.Precision.HIGHEST,
        )
        sketches.append(sketch * (1.0 / math.sqrt(LEN)))
    stacked = jnp.stack(sketches, axis=1).reshape(seq_count, layer_count * rank_size * rank_size)
    stacked = stacked.astype(jnp.bfloat16)
    score_scale = 1.0 / math.sqrt(layer_count * rank_size * rank_size)
    product = lax.dot_general(
        query_sketch,
        lax.all_gather(stacked, "dp", axis=0, tiled=True),
        (((1,), (1,)), ((), ())),
        preferred_element_type=jnp.float32,
    )
    return product * score_scale


def fused_kernel(
    n, len_ref, hid_ref, grad_ref, fac_ref, pout_ref, query_ref, out_ref,
    hid, grad, pout, query, held, turned, sketches, spread,
    load_sem, ring_send, ring_recv, pair_send, pair_recv, sk_send, sk_recv,
):
    layers, rank, depth = fac_ref.shape
    chips = n // 2
    half = chips // 2
    row_half = rank // 2
    me = lax.axis_index("dp")
    core = me % 2
    chip = me // 2
    odd = chip % 2
    place = (1 - odd) * (chip // 2) + odd * (chips - 1 - chip // 2)

    def device_at(spot, which):
        spot = lax.rem(spot + 2 * chips, chips)
        upper = spot // half
        return 2 * ((1 - upper) * 2 * spot + upper * (2 * (chips - 1 - spot) + 1)) + which

    up = device_at(place + 1, core)
    down = device_at(place - 1, core)
    pair = me + 1 - 2 * core

    loads = []

    def load(src, dst):
        copy = pltpu.make_async_copy(src, dst, load_sem.at[len(loads)])
        copy.start()
        loads.append(copy)
        return copy

    barrier = pltpu.get_barrier_semaphore()
    for step in range(1, n):
        pl.semaphore_signal(
            barrier, inc=1, device_id={"dp": lax.rem(me + step, n)}, device_id_type=MESH
        )
    load_grad = load(grad_ref, grad)
    load_pout = load(pout_ref, pout)
    load_own = load(fac_ref, held.at[:, 0, 0])
    load_hid = [load(hid_ref.at[layer], hid.at[layer]) for layer in range(layers)]
    load_query = load(query_ref, query)
    pl.semaphore_wait(barrier, n - 1)

    sent = []

    def send(src, dst, send_sem, recv_sem, device):
        copy = pltpu.make_async_remote_copy(
            src_ref=src, dst_ref=dst, send_sem=send_sem, recv_sem=recv_sem,
            device_id={"dp": device}, device_id_type=MESH,
        )
        copy.start()
        sent.append(copy)
        return copy

    def rows_of(slot):
        if slot == chips:
            return half, pl.ds(row_half, rank - row_half)
        if slot == half:
            return half, pl.ds(0, row_half)
        return slot, pl.ds(0, rank)

    def ring(layer, src, slot, device):
        where, rows = rows_of(slot)
        return send(
            src.at[rows], held.at[layer, 0, where, rows],
            ring_send.at[layer, slot], ring_recv.at[layer, slot], device,
        )

    def across(layer, slot):
        where, rows = rows_of(slot)
        return send(
            held.at[layer, 0, where, rows], held.at[layer, 1, where, rows],
            pair_send.at[layer, slot], pair_recv.at[layer, slot], pair,
        )

    def arrived(layer, bank, slot):
        where, rows = rows_of(slot)
        ref = held.at[layer, bank, where, rows]
        sems = (pair_send, pair_recv) if bank else (ring_send, ring_recv)
        pltpu.make_async_remote_copy(
            src_ref=ref, dst_ref=ref, send_sem=sems[0].at[layer, slot], recv_sem=sems[1].at[layer, slot],
            device_id={"dp": pair}, device_id_type=MESH,
        ).wait_recv()

    for layer in range(layers):
        ring(layer, fac_ref.at[layer], 1, up)
        ring(layer, fac_ref.at[layer], chips - 1, down)
    load_own.wait()
    for layer in range(layers):
        across(layer, 0)

    load_grad.wait()
    load_pout.wait()
    count = len_ref[0]
    kept = (lax.broadcasted_iota(jnp.int32, (rank, LEN), 1) < count).astype(jnp.float32)
    left = []
    for layer in range(layers):
        turned[layer] = kept * lax.dot_general(
            pout[layer], grad[layer], ROWS_BY_ROWS, preferred_element_type=jnp.float32
        )
        left.append(jnp.concatenate(
            [turned[layer, pl.ds(0, rank // 2, stride=2), :], turned[layer, pl.ds(1, rank // 2, stride=2), :]],
            axis=0,
        ))

    totals = [jnp.zeros((LEN, rank), jnp.float32) for _ in range(layers)]

    def add(layer, bank, slot):
        owner = device_at(place - slot, core if bank == 0 else 1 - core)
        columns = pl.ds(pl.multiple_of(owner * depth, depth), depth)
        totals[layer] += lax.dot_general(
            hid[layer, :, columns], held[layer, bank, slot], ROWS_BY_ROWS, preferred_element_type=jnp.float32
        )

    def finish(layer):
        sketch = lax.dot_general(
            left[layer], totals[layer], (((1,), (0,)), ((), ())),
            precision=lax.Precision.HIGHEST, preferred_element_type=jnp.float32,
        ) * (1.0 / math.sqrt(LEN))
        flat = jnp.concatenate([sketch[: rank // 2], sketch[rank // 2 :]], axis=1)
        sketches[layer, me] = flat.astype(jnp.bfloat16)
        for step in range(1, n):
            send(
                sketches.at[layer, me], sketches.at[layer, me],
                sk_send.at[layer, step], sk_recv.at[layer, step], lax.rem(me + step, n),
            )

    for layer in range(layers):
        load_hid[layer].wait()
        add(layer, 0, 0)
    for hop in range(1, half + 1):
        for layer in range(layers):
            if hop < half:
                arrived(layer, 0, hop)
                ring(layer, held.at[layer, 0, hop], hop + 1, up)
                across(layer, hop)
                arrived(layer, 0, chips - hop)
                ring(layer, held.at[layer, 0, chips - hop], chips - hop - 1 if hop + 1 < half else chips, down)
                across(layer, chips - hop)
                add(layer, 0, hop)
                add(layer, 0, chips - hop)
            else:
                arrived(layer, 0, half)
                across(layer, half)
                arrived(layer, 0, chips)
                across(layer, chips)
                add(layer, 0, half)
            if hop == 1:
                arrived(layer, 1, 0)
                add(layer, 1, 0)
            else:
                for slot in (hop - 1, chips - hop + 1):
                    arrived(layer, 1, slot)
                    add(layer, 1, slot)
            if hop == half:
                arrived(layer, 1, half)
                arrived(layer, 1, chips)
                add(layer, 1, half)
                finish(layer)

    load_query.wait()
    scores = jnp.zeros((query.shape[0], n), jnp.float32)
    width = rank * rank
    for layer in range(layers):
        for step in range(1, n):
            ref = sketches.at[layer, lax.rem(me + n - step, n)]
            pltpu.make_async_remote_copy(
                src_ref=ref, dst_ref=ref, send_sem=sk_send.at[layer, step], recv_sem=sk_recv.at[layer, step],
                device_id={"dp": pair}, device_id_type=MESH,
            ).wait_recv()
        lines = width // 128
        spread[...] = sketches[layer].astype(jnp.float32).reshape(n * lines, 128)
        flat = jnp.concatenate(
            [spread[pl.ds(line, n, stride=lines), :].astype(jnp.bfloat16) for line in range(lines)], axis=1
        )
        scores += lax.dot_general(
            query[:, layer * width : (layer + 1) * width], flat, ROWS_BY_ROWS, preferred_element_type=jnp.float32
        )
    out_ref[...] = scores * (1.0 / math.sqrt(layers * width))
    for copy in sent:
        copy.wait_send()


def fused(n, hidden_in, out_grad, proj_hidden, proj_out, lengths, query_sketch):
    layers, tokens, hidden = hidden_in.shape
    depth, rank = proj_hidden.shape[1:]
    queries = query_sketch.shape[0]
    lines = rank * rank // 128
    slots = n // 2 + 1
    dma = pltpu.SemaphoreType.DMA
    return pl.pallas_call(
        functools.partial(fused_kernel, n),
        out_shape=jax.ShapeDtypeStruct((queries, n), jnp.float32),
        in_specs=[pl.BlockSpec(memory_space=pltpu.SMEM)] + [pl.BlockSpec(memory_space=pl.ANY)] * 5,
        out_specs=pl.BlockSpec(memory_space=pltpu.VMEM),
        scratch_shapes=[
            pltpu.VMEM((layers, tokens, hidden), jnp.bfloat16),
            pltpu.VMEM(out_grad.shape, jnp.bfloat16),
            pltpu.VMEM((layers, rank, proj_out.shape[1]), jnp.bfloat16),
            pltpu.VMEM(query_sketch.shape, jnp.bfloat16),
            pltpu.VMEM((layers, 2, n // 2, rank, depth), jnp.bfloat16),
            pltpu.VMEM((layers, rank, LEN), jnp.float32),
            pltpu.VMEM((layers, n, lines, 128), jnp.bfloat16),
            pltpu.VMEM((n * lines, 128), jnp.float32),
            dma((8,)),
            dma((layers, slots)),
            dma((layers, slots)),
            dma((layers, slots)),
            dma((layers, slots)),
            dma((layers, n)),
            dma((layers, n)),
        ],
        compiler_params=pltpu.CompilerParams(
            collective_id=0, has_side_effects=True, vmem_limit_bytes=48 << 20
        ),
        cost_estimate=pl.CostEstimate(
            flops=2 * layers * tokens * rank * (hidden + out_grad.shape[2]),
            bytes_accessed=2 * layers * tokens * (hidden + out_grad.shape[2]),
            transcendentals=0,
        ),
    )(
        lengths, hidden_in, out_grad, jnp.swapaxes(proj_hidden, 1, 2), jnp.swapaxes(proj_out, 1, 2), query_sketch
    )


def solution(mesh):
    n = mesh.shape["dp"]

    def on_device(hidden_in, out_grad, proj_hidden, proj_out, lengths, query_sketch):
        args = (hidden_in, out_grad, proj_hidden, proj_out, lengths, query_sketch)
        aligned = proj_hidden.shape[1] % 128 == 0 and proj_hidden.shape[2] == 64
        if aligned and lengths.shape[0] == 1 and out_grad.shape[1] == LEN and n % 4 == 0 and n >= 8:
            return fused(n, *args)
        return plain(*args)

    return jax.shard_map(
        on_device,
        mesh=mesh,
        in_specs=(
            P(None, ("groups", "dp"), None),
            P(None, ("groups", "dp"), None),
            P(None, "dp", None),
            P(),
            P(("groups", "dp")),
            P(("groups", "dp"), None),
        ),
        out_specs=P(("groups", "dp"), None),
        check_vma=False,
    )
```

```python
import functools
import math

import jax
import jax.numpy as jnp
from jax import lax
from jax.experimental import pallas as pl
from jax.experimental.pallas import tpu as pltpu
from jax.sharding import PartitionSpec as P

LEN = 128
MESH = pl.DeviceIdType.MESH
ROWS_BY_ROWS = (((1,), (1,)), ((), ()))


def plain(hidden_in, out_grad, proj_hidden, proj_out, lengths, query_sketch):
    layer_count = hidden_in.shape[0]
    rank_size = proj_out.shape[2]
    tok_rows = out_grad.shape[1]
    seq_count = lengths.shape[0]
    position = jnp.arange(tok_rows, dtype=jnp.int32)
    length_limit = jnp.repeat(lengths, LEN)
    kept_mask = (position % LEN < length_limit).astype(jnp.float32)
    inputs = jnp.einsum(
        "lth,lhr->ltr",
        hidden_in,
        lax.all_gather(proj_hidden, "dp", axis=1, tiled=True),
        preferred_element_type=jnp.float32,
    )
    sketches = []
    for layer in range(layer_count):
        projected_out = jnp.dot(
            out_grad[layer], proj_out[layer], preferred_element_type=jnp.float32
        )
        projected_out = projected_out * kept_mask[:, None]
        sketch = jnp.einsum(
            "epa,epb->eab",
            projected_out.reshape(seq_count, LEN, rank_size),
            inputs[layer].reshape(seq_count, LEN, rank_size),
            precision=lax.Precision.HIGHEST,
        )
        sketches.append(sketch * (1.0 / math.sqrt(LEN)))
    stacked = jnp.stack(sketches, axis=1).reshape(seq_count, layer_count * rank_size * rank_size)
    stacked = stacked.astype(jnp.bfloat16)
    score_scale = 1.0 / math.sqrt(layer_count * rank_size * rank_size)
    product = lax.dot_general(
        query_sketch,
        lax.all_gather(stacked, "dp", axis=0, tiled=True),
        (((1,), (1,)), ((), ())),
        preferred_element_type=jnp.float32,
    )
    return product * score_scale


def fused_kernel(
    n, len_ref, hid_ref, grad_ref, fac_ref, pout_ref, query_ref, out_ref,
    hid, grad, pout, query, held, turned, sketches, spread,
    load_sem, ring_send, ring_recv, pair_send, pair_recv, sk_send, sk_recv,
):
    layers, rank, depth = fac_ref.shape
    chips = n // 2
    half = chips // 2
    row_half = rank // 2
    me = lax.axis_index("dp")
    core = me % 2
    chip = me // 2
    odd = chip % 2
    place = (1 - odd) * (chip // 2) + odd * (chips - 1 - chip // 2)

    def device_at(spot, which):
        spot = lax.rem(spot + 2 * chips, chips)
        upper = spot // half
        return 2 * ((1 - upper) * 2 * spot + upper * (2 * (chips - 1 - spot) + 1)) + which

    up = device_at(place + 1, core)
    down = device_at(place - 1, core)
    pair = me + 1 - 2 * core

    loads = []

    def load(src, dst):
        copy = pltpu.make_async_copy(src, dst, load_sem.at[len(loads)])
        copy.start()
        loads.append(copy)
        return copy

    barrier = pltpu.get_barrier_semaphore()
    for other in (up, down, pair):
        pl.semaphore_signal(barrier, inc=1, device_id={"dp": other}, device_id_type=MESH)
    load_grad = load(grad_ref, grad)
    load_pout = load(pout_ref, pout)
    load_own = load(fac_ref, held.at[:, 0, 0])
    load_hid = [load(hid_ref.at[layer], hid.at[layer]) for layer in range(layers)]
    load_query = load(query_ref, query)
    pl.semaphore_wait(barrier, 3)

    sent = []

    def send(src, dst, send_sem, recv_sem, device):
        copy = pltpu.make_async_remote_copy(
            src_ref=src, dst_ref=dst, send_sem=send_sem, recv_sem=recv_sem,
            device_id={"dp": device}, device_id_type=MESH,
        )
        copy.start()
        sent.append(copy)
        return copy

    def rows_of(slot):
        if slot == chips:
            return half, pl.ds(row_half, rank - row_half)
        if slot == half:
            return half, pl.ds(0, row_half)
        return slot, pl.ds(0, rank)

    def ring(layer, src, slot, device):
        where, rows = rows_of(slot)
        return send(
            src.at[rows], held.at[layer, 0, where, rows],
            ring_send.at[layer, slot], ring_recv.at[layer, slot], device,
        )

    def across(layer, slot):
        where, rows = rows_of(slot)
        return send(
            held.at[layer, 0, where, rows], held.at[layer, 1, where, rows],
            pair_send.at[layer, slot], pair_recv.at[layer, slot], pair,
        )

    def arrived(layer, bank, slot):
        where, rows = rows_of(slot)
        ref = held.at[layer, bank, where, rows]
        sems = (pair_send, pair_recv) if bank else (ring_send, ring_recv)
        pltpu.make_async_remote_copy(
            src_ref=ref, dst_ref=ref, send_sem=sems[0].at[layer, slot], recv_sem=sems[1].at[layer, slot],
            device_id={"dp": pair}, device_id_type=MESH,
        ).wait_recv()

    for layer in range(layers):
        ring(layer, fac_ref.at[layer], 1, up)
        ring(layer, fac_ref.at[layer], chips - 1, down)
    load_own.wait()
    for layer in range(layers):
        across(layer, 0)

    load_grad.wait()
    load_pout.wait()
    count = len_ref[0]
    kept = (lax.broadcasted_iota(jnp.int32, (rank, LEN), 1) < count).astype(jnp.float32)
    left = []
    for layer in range(layers):
        turned[layer] = kept * lax.dot_general(
            pout[layer], grad[layer], ROWS_BY_ROWS, preferred_element_type=jnp.float32
        )
        left.append(jnp.concatenate(
            [turned[layer, pl.ds(0, rank // 2, stride=2), :], turned[layer, pl.ds(1, rank // 2, stride=2), :]],
            axis=0,
        ))

    totals = [jnp.zeros((LEN, rank), jnp.float32) for _ in range(layers)]

    def add(layer, bank, slot):
        owner = device_at(place - slot, core if bank == 0 else 1 - core)
        columns = pl.ds(pl.multiple_of(owner * depth, depth), depth)
        totals[layer] += lax.dot_general(
            hid[layer, :, columns], held[layer, bank, slot], ROWS_BY_ROWS, preferred_element_type=jnp.float32
        )

    def finish(layer):
        sketch = lax.dot_general(
            left[layer], totals[layer], (((1,), (0,)), ((), ())),
            precision=lax.Precision.HIGHEST, preferred_element_type=jnp.float32,
        ) * (1.0 / math.sqrt(LEN))
        flat = jnp.concatenate([sketch[: rank // 2], sketch[rank // 2 :]], axis=1)
        sketches[layer, me] = flat.astype(jnp.bfloat16)
        for step in range(1, n):
            send(
                sketches.at[layer, me], sketches.at[layer, me],
                sk_send.at[layer, step], sk_recv.at[layer, step], lax.rem(me + step, n),
            )

    for layer in range(layers):
        load_hid[layer].wait()
        add(layer, 0, 0)
    for hop in range(1, half + 1):
        for layer in range(layers):
            if hop < half:
                arrived(layer, 0, hop)
                ring(layer, held.at[layer, 0, hop], hop + 1, up)
                across(layer, hop)
                arrived(layer, 0, chips - hop)
                ring(layer, held.at[layer, 0, chips - hop], chips - hop - 1 if hop + 1 < half else chips, down)
                across(layer, chips - hop)
                add(layer, 0, hop)
                add(layer, 0, chips - hop)
            else:
                arrived(layer, 0, half)
                across(layer, half)
                arrived(layer, 0, chips)
                across(layer, chips)
                add(layer, 0, half)
            if hop == 1:
                arrived(layer, 1, 0)
                add(layer, 1, 0)
            else:
                for slot in (hop - 1, chips - hop + 1):
                    arrived(layer, 1, slot)
                    add(layer, 1, slot)
            if hop == half:
                arrived(layer, 1, half)
                arrived(layer, 1, chips)
                add(layer, 1, half)
                finish(layer)

    load_query.wait()
    scores = jnp.zeros((query.shape[0], n), jnp.float32)
    width = rank * rank
    for layer in range(layers):
        for step in range(1, n):
            ref = sketches.at[layer, lax.rem(me + n - step, n)]
            pltpu.make_async_remote_copy(
                src_ref=ref, dst_ref=ref, send_sem=sk_send.at[layer, step], recv_sem=sk_recv.at[layer, step],
                device_id={"dp": pair}, device_id_type=MESH,
            ).wait_recv()
        lines = width // 128
        spread[...] = sketches[layer].astype(jnp.float32).reshape(n * lines, 128)
        flat = jnp.concatenate(
            [spread[pl.ds(line, n, stride=lines), :].astype(jnp.bfloat16) for line in range(lines)], axis=1
        )
        scores += lax.dot_general(
            query[:, layer * width : (layer + 1) * width], flat, ROWS_BY_ROWS, preferred_element_type=jnp.float32
        )
    out_ref[...] = scores * (1.0 / math.sqrt(layers * width))
    for copy in sent:
        copy.wait_send()


def fused(n, hidden_in, out_grad, proj_hidden, proj_out, lengths, query_sketch):
    layers, tokens, hidden = hidden_in.shape
    depth, rank = proj_hidden.shape[1:]
    queries = query_sketch.shape[0]
    lines = rank * rank // 128
    slots = n // 2 + 1
    dma = pltpu.SemaphoreType.DMA
    return pl.pallas_call(
        functools.partial(fused_kernel, n),
        out_shape=jax.ShapeDtypeStruct((queries, n), jnp.float32),
        in_specs=[pl.BlockSpec(memory_space=pltpu.SMEM)] + [pl.BlockSpec(memory_space=pl.ANY)] * 5,
        out_specs=pl.BlockSpec(memory_space=pltpu.VMEM),
        scratch_shapes=[
            pltpu.VMEM((layers, tokens, hidden), jnp.bfloat16),
            pltpu.VMEM(out_grad.shape, jnp.bfloat16),
            pltpu.VMEM((layers, rank, proj_out.shape[1]), jnp.bfloat16),
            pltpu.VMEM(query_sketch.shape, jnp.bfloat16),
            pltpu.VMEM((layers, 2, n // 2, rank, depth), jnp.bfloat16),
            pltpu.VMEM((layers, rank, LEN), jnp.float32),
            pltpu.VMEM((layers, n, lines, 128), jnp.bfloat16),
            pltpu.VMEM((n * lines, 128), jnp.float32),
            dma((8,)),
            dma((layers, slots)),
            dma((layers, slots)),
            dma((layers, slots)),
            dma((layers, slots)),
            dma((layers, n)),
            dma((layers, n)),
        ],
        compiler_params=pltpu.CompilerParams(
            collective_id=0, has_side_effects=True, vmem_limit_bytes=63 << 20
        ),
        cost_estimate=pl.CostEstimate(
            flops=2 * layers * tokens * rank * (hidden + out_grad.shape[2]),
            bytes_accessed=2 * layers * tokens * (hidden + out_grad.shape[2]),
            transcendentals=0,
        ),
    )(
        lengths, hidden_in, out_grad, jnp.swapaxes(proj_hidden, 1, 2), jnp.swapaxes(proj_out, 1, 2), query_sketch
    )


def solution(mesh):
    n = mesh.shape["dp"]

    def on_device(hidden_in, out_grad, proj_hidden, proj_out, lengths, query_sketch):
        args = (hidden_in, out_grad, proj_hidden, proj_out, lengths, query_sketch)
        aligned = proj_hidden.shape[1] % 128 == 0 and proj_hidden.shape[2] == 64
        if aligned and lengths.shape[0] == 1 and out_grad.shape[1] == LEN and n % 4 == 0 and n >= 8:
            return fused(n, *args)
        return plain(*args)

    return jax.shard_map(
        on_device,
        mesh=mesh,
        in_specs=(
            P(None, ("groups", "dp"), None),
            P(None, ("groups", "dp"), None),
            P(None, "dp", None),
            P(),
            P(("groups", "dp")),
            P(("groups", "dp"), None),
        ),
        out_specs=P(("groups", "dp"), None),
        check_vma=False,
    )
```

```python
import functools
import math

import jax
import jax.numpy as jnp
from jax import lax
from jax.experimental import pallas as pl
from jax.experimental.pallas import tpu as pltpu
from jax.sharding import PartitionSpec as P

LEN = 128
MESH = pl.DeviceIdType.MESH
RELAYED = (0,)
ROWS_BY_ROWS = (((1,), (1,)), ((), ()))


def plain(hidden_in, out_grad, proj_hidden, proj_out, lengths, query_sketch):
    layer_count = hidden_in.shape[0]
    rank_size = proj_out.shape[2]
    tok_rows = out_grad.shape[1]
    seq_count = lengths.shape[0]
    position = jnp.arange(tok_rows, dtype=jnp.int32)
    length_limit = jnp.repeat(lengths, LEN)
    kept_mask = (position % LEN < length_limit).astype(jnp.float32)
    inputs = jnp.einsum(
        "lth,lhr->ltr",
        hidden_in,
        lax.all_gather(proj_hidden, "dp", axis=1, tiled=True),
        preferred_element_type=jnp.float32,
    )
    sketches = []
    for layer in range(layer_count):
        projected_out = jnp.dot(
            out_grad[layer], proj_out[layer], preferred_element_type=jnp.float32
        )
        projected_out = projected_out * kept_mask[:, None]
        sketch = jnp.einsum(
            "epa,epb->eab",
            projected_out.reshape(seq_count, LEN, rank_size),
            inputs[layer].reshape(seq_count, LEN, rank_size),
            precision=lax.Precision.HIGHEST,
        )
        sketches.append(sketch * (1.0 / math.sqrt(LEN)))
    stacked = jnp.stack(sketches, axis=1).reshape(seq_count, layer_count * rank_size * rank_size)
    stacked = stacked.astype(jnp.bfloat16)
    score_scale = 1.0 / math.sqrt(layer_count * rank_size * rank_size)
    product = lax.dot_general(
        query_sketch,
        lax.all_gather(stacked, "dp", axis=0, tiled=True),
        (((1,), (1,)), ((), ())),
        preferred_element_type=jnp.float32,
    )
    return product * score_scale


def fused_kernel(
    n, len_ref, hid_ref, grad_ref, fac_ref, pout_ref, query_ref, out_ref,
    hid, grad, pout, query, held, turned, sketches, spread,
    load_sem, ring_send, ring_recv, pair_send, pair_recv, sk_send, sk_recv,
):
    layers, rank, depth = fac_ref.shape
    chips = n // 2
    half = chips // 2
    row_half = rank // 2
    me = lax.axis_index("dp")
    core = me % 2
    chip = me // 2
    odd = chip % 2
    place = (1 - odd) * (chip // 2) + odd * (chips - 1 - chip // 2)

    def device_at(spot, which):
        spot = lax.rem(spot + 2 * chips, chips)
        upper = spot // half
        return 2 * ((1 - upper) * 2 * spot + upper * (2 * (chips - 1 - spot) + 1)) + which

    up = device_at(place + 1, core)
    down = device_at(place - 1, core)
    pair = me + 1 - 2 * core

    loads = []

    def load(src, dst):
        copy = pltpu.make_async_copy(src, dst, load_sem.at[len(loads)])
        copy.start()
        loads.append(copy)
        return copy

    barrier = pltpu.get_barrier_semaphore()
    for other in (up, down, pair):
        pl.semaphore_signal(barrier, inc=1, device_id={"dp": other}, device_id_type=MESH)
    load_grad = load(grad_ref, grad)
    load_pout = load(pout_ref, pout)
    load_own = load(fac_ref, held.at[:, 0, 0])
    load_hid = [load(hid_ref.at[layer], hid.at[layer]) for layer in range(layers)]
    load_query = load(query_ref, query)
    pl.semaphore_wait(barrier, 3)

    sent = []

    def send(src, dst, send_sem, recv_sem, device):
        copy = pltpu.make_async_remote_copy(
            src_ref=src, dst_ref=dst, send_sem=send_sem, recv_sem=recv_sem,
            device_id={"dp": device}, device_id_type=MESH,
        )
        copy.start()
        sent.append(copy)
        return copy

    def rows_of(slot):
        if slot == chips:
            return half, pl.ds(row_half, rank - row_half)
        if slot == half:
            return half, pl.ds(0, row_half)
        return slot, pl.ds(0, rank)

    def ring(layer, src, slot, device):
        where, rows = rows_of(slot)
        return send(
            src.at[rows], held.at[layer, 0, where, rows],
            ring_send.at[layer, slot], ring_recv.at[layer, slot], device,
        )

    def across(layer, slot):
        where, rows = rows_of(slot)
        return send(
            held.at[layer, 0, where, rows], held.at[layer, 1, where, rows],
            pair_send.at[layer, slot], pair_recv.at[layer, slot], pair,
        )

    def arrived(layer, bank, slot):
        where, rows = rows_of(slot)
        ref = held.at[layer, bank, where, rows]
        sems = (pair_send, pair_recv) if bank else (ring_send, ring_recv)
        pltpu.make_async_remote_copy(
            src_ref=ref, dst_ref=ref, send_sem=sems[0].at[layer, slot], recv_sem=sems[1].at[layer, slot],
            device_id={"dp": pair}, device_id_type=MESH,
        ).wait_recv()

    for layer in range(layers):
        ring(layer, fac_ref.at[layer], 1, up)
        ring(layer, fac_ref.at[layer], chips - 1, down)
    load_own.wait()
    for layer in range(layers):
        across(layer, 0)

    load_grad.wait()
    load_pout.wait()
    count = len_ref[0]
    kept = (lax.broadcasted_iota(jnp.int32, (rank, LEN), 1) < count).astype(jnp.float32)
    left = []
    for layer in range(layers):
        turned[layer] = kept * lax.dot_general(
            pout[layer], grad[layer], ROWS_BY_ROWS, preferred_element_type=jnp.float32
        )
        left.append(jnp.concatenate(
            [turned[layer, pl.ds(0, rank // 2, stride=2), :], turned[layer, pl.ds(1, rank // 2, stride=2), :]],
            axis=0,
        ))

    totals = [jnp.zeros((LEN, rank), jnp.float32) for _ in range(layers)]

    def add(layer, bank, slot):
        owner = device_at(place - slot, core if bank == 0 else 1 - core)
        columns = pl.ds(pl.multiple_of(owner * depth, depth), depth)
        totals[layer] += lax.dot_general(
            hid[layer, :, columns], held[layer, bank, slot], ROWS_BY_ROWS, preferred_element_type=jnp.float32
        )

    def finish(layer):
        sketch = lax.dot_general(
            left[layer], totals[layer], (((1,), (0,)), ((), ())),
            precision=lax.Precision.HIGHEST, preferred_element_type=jnp.float32,
        ) * (1.0 / math.sqrt(LEN))
        flat = jnp.concatenate([sketch[: rank // 2], sketch[rank // 2 :]], axis=1)
        sketches[layer, me] = flat.astype(jnp.bfloat16)
        mine = sketches.at[layer, me]
        if layer in RELAYED:
            send(mine, mine, sk_send.at[layer, 1], sk_recv.at[layer, 1], pair)
        for step in range(2, n, 2) if layer in RELAYED else range(1, n):
            send(mine, mine, sk_send.at[layer, step], sk_recv.at[layer, step], lax.rem(me + step, n))

    for layer in range(layers):
        load_hid[layer].wait()
        add(layer, 0, 0)
    for hop in range(1, half + 1):
        for layer in range(layers):
            if hop < half:
                arrived(layer, 0, hop)
                ring(layer, held.at[layer, 0, hop], hop + 1, up)
                across(layer, hop)
                arrived(layer, 0, chips - hop)
                ring(layer, held.at[layer, 0, chips - hop], chips - hop - 1 if hop + 1 < half else chips, down)
                across(layer, chips - hop)
                add(layer, 0, hop)
                add(layer, 0, chips - hop)
            else:
                arrived(layer, 0, half)
                across(layer, half)
                arrived(layer, 0, chips)
                across(layer, chips)
                add(layer, 0, half)
            if hop == 1:
                arrived(layer, 1, 0)
                add(layer, 1, 0)
            else:
                for slot in (hop - 1, chips - hop + 1):
                    arrived(layer, 1, slot)
                    add(layer, 1, slot)
            if hop == half:
                arrived(layer, 1, half)
                arrived(layer, 1, chips)
                add(layer, 1, half)
                finish(layer)

    def sketch_arrived(layer, step, source):
        ref = sketches.at[layer, lax.rem(source, n)]
        pltpu.make_async_remote_copy(
            src_ref=ref, dst_ref=ref, send_sem=sk_send.at[layer, step], recv_sem=sk_recv.at[layer, step],
            device_id={"dp": pair}, device_id_type=MESH,
        ).wait_recv()
        return ref

    for layer in RELAYED:
        for step in range(2, n, 2):
            ref = sketch_arrived(layer, step, me + n - step)
            send(ref, ref, sk_send.at[layer, step + 1], sk_recv.at[layer, step + 1], pair)

    load_query.wait()
    scores = jnp.zeros((query.shape[0], n), jnp.float32)
    width = rank * rank
    for layer in range(layers):
        if layer in RELAYED:
            for step in range(0, n, 2):
                sketch_arrived(layer, step + 1, pair + n - step)
        else:
            for step in range(1, n):
                sketch_arrived(layer, step, me + n - step)
        lines = width // 128
        spread[...] = sketches[layer].astype(jnp.float32).reshape(n * lines, 128)
        flat = jnp.concatenate(
            [spread[pl.ds(line, n, stride=lines), :].astype(jnp.bfloat16) for line in range(lines)], axis=1
        )
        scores += lax.dot_general(
            query[:, layer * width : (layer + 1) * width], flat, ROWS_BY_ROWS, preferred_element_type=jnp.float32
        )
    out_ref[...] = scores * (1.0 / math.sqrt(layers * width))
    for copy in sent:
        copy.wait_send()


def fused(n, hidden_in, out_grad, proj_hidden, proj_out, lengths, query_sketch):
    layers, tokens, hidden = hidden_in.shape
    depth, rank = proj_hidden.shape[1:]
    queries = query_sketch.shape[0]
    lines = rank * rank // 128
    slots = n // 2 + 1
    dma = pltpu.SemaphoreType.DMA
    return pl.pallas_call(
        functools.partial(fused_kernel, n),
        out_shape=jax.ShapeDtypeStruct((queries, n), jnp.float32),
        in_specs=[pl.BlockSpec(memory_space=pltpu.SMEM)] + [pl.BlockSpec(memory_space=pl.ANY)] * 5,
        out_specs=pl.BlockSpec(memory_space=pltpu.VMEM),
        scratch_shapes=[
            pltpu.VMEM((layers, tokens, hidden), jnp.bfloat16),
            pltpu.VMEM(out_grad.shape, jnp.bfloat16),
            pltpu.VMEM((layers, rank, proj_out.shape[1]), jnp.bfloat16),
            pltpu.VMEM(query_sketch.shape, jnp.bfloat16),
            pltpu.VMEM((layers, 2, n // 2, rank, depth), jnp.bfloat16),
            pltpu.VMEM((layers, rank, LEN), jnp.float32),
            pltpu.VMEM((layers, n, lines, 128), jnp.bfloat16),
            pltpu.VMEM((n * lines, 128), jnp.float32),
            dma((8,)),
            dma((layers, slots)),
            dma((layers, slots)),
            dma((layers, slots)),
            dma((layers, slots)),
            dma((layers, n)),
            dma((layers, n)),
        ],
        compiler_params=pltpu.CompilerParams(
            collective_id=0, has_side_effects=True, vmem_limit_bytes=63 << 20
        ),
        cost_estimate=pl.CostEstimate(
            flops=2 * layers * tokens * rank * (hidden + out_grad.shape[2]),
            bytes_accessed=2 * layers * tokens * (hidden + out_grad.shape[2]),
            transcendentals=0,
        ),
    )(
        lengths, hidden_in, out_grad, jnp.swapaxes(proj_hidden, 1, 2), jnp.swapaxes(proj_out, 1, 2), query_sketch
    )


def solution(mesh):
    n = mesh.shape["dp"]

    def on_device(hidden_in, out_grad, proj_hidden, proj_out, lengths, query_sketch):
        args = (hidden_in, out_grad, proj_hidden, proj_out, lengths, query_sketch)
        aligned = proj_hidden.shape[1] % 128 == 0 and proj_hidden.shape[2] == 64
        if aligned and lengths.shape[0] == 1 and out_grad.shape[1] == LEN and n % 4 == 0 and n >= 8:
            return fused(n, *args)
        return plain(*args)

    return jax.shard_map(
        on_device,
        mesh=mesh,
        in_specs=(
            P(None, ("groups", "dp"), None),
            P(None, ("groups", "dp"), None),
            P(None, "dp", None),
            P(),
            P(("groups", "dp")),
            P(("groups", "dp"), None),
        ),
        out_specs=P(("groups", "dp"), None),
        check_vma=False,
    )
```

```python
import functools
import math

import jax
import jax.numpy as jnp
from jax import lax
from jax.experimental import pallas as pl
from jax.experimental.pallas import tpu as pltpu
from jax.sharding import PartitionSpec as P

LEN = 128
MESH = pl.DeviceIdType.MESH
RELAYED = (0,)
ROWS_BY_ROWS = (((1,), (1,)), ((), ()))


def plain(hidden_in, out_grad, proj_hidden, proj_out, lengths, query_sketch):
    layer_count = hidden_in.shape[0]
    rank_size = proj_out.shape[2]
    tok_rows = out_grad.shape[1]
    seq_count = lengths.shape[0]
    position = jnp.arange(tok_rows, dtype=jnp.int32)
    length_limit = jnp.repeat(lengths, LEN)
    kept_mask = (position % LEN < length_limit).astype(jnp.float32)
    inputs = jnp.einsum(
        "lth,lhr->ltr",
        hidden_in,
        lax.all_gather(proj_hidden, "dp", axis=1, tiled=True),
        preferred_element_type=jnp.float32,
    )
    sketches = []
    for layer in range(layer_count):
        projected_out = jnp.dot(
            out_grad[layer], proj_out[layer], preferred_element_type=jnp.float32
        )
        projected_out = projected_out * kept_mask[:, None]
        sketch = jnp.einsum(
            "epa,epb->eab",
            projected_out.reshape(seq_count, LEN, rank_size),
            inputs[layer].reshape(seq_count, LEN, rank_size),
            precision=lax.Precision.HIGHEST,
        )
        sketches.append(sketch * (1.0 / math.sqrt(LEN)))
    stacked = jnp.stack(sketches, axis=1).reshape(seq_count, layer_count * rank_size * rank_size)
    stacked = stacked.astype(jnp.bfloat16)
    score_scale = 1.0 / math.sqrt(layer_count * rank_size * rank_size)
    product = lax.dot_general(
        query_sketch,
        lax.all_gather(stacked, "dp", axis=0, tiled=True),
        (((1,), (1,)), ((), ())),
        preferred_element_type=jnp.float32,
    )
    return product * score_scale


def fused_kernel(
    n, len_ref, hid_ref, grad_ref, fac_ref, pout_ref, query_ref, out_ref,
    hid, grad, pout, query, held, turned, sketches, spread,
    load_sem, ring_send, ring_recv, pair_send, pair_recv, sk_send, sk_recv,
):
    layers, rank, depth = fac_ref.shape
    chips = n // 2
    half = chips // 2
    row_half = rank // 2
    me = lax.axis_index("dp")
    core = me % 2
    chip = me // 2
    odd = chip % 2
    place = (1 - odd) * (chip // 2) + odd * (chips - 1 - chip // 2)

    def device_at(spot, which):
        spot = lax.rem(spot + 2 * chips, chips)
        upper = spot // half
        return 2 * ((1 - upper) * 2 * spot + upper * (2 * (chips - 1 - spot) + 1)) + which

    up = device_at(place + 1, core)
    down = device_at(place - 1, core)
    pair = me + 1 - 2 * core

    loads = []

    def load(src, dst):
        copy = pltpu.make_async_copy(src, dst, load_sem.at[len(loads)])
        copy.start()
        loads.append(copy)
        return copy

    barrier = pltpu.get_barrier_semaphore()
    for other in (up, down, pair):
        pl.semaphore_signal(barrier, inc=1, device_id={"dp": other}, device_id_type=MESH)
    load_own = load(fac_ref, held.at[:, 0, 0])
    load_grad = load(grad_ref, grad)
    load_pout = load(pout_ref, pout)
    load_hid = [load(hid_ref.at[layer], hid.at[layer]) for layer in range(layers)]
    load_query = load(query_ref, query)
    pl.semaphore_wait(barrier, 3)

    sent = []

    def send(src, dst, send_sem, recv_sem, device):
        copy = pltpu.make_async_remote_copy(
            src_ref=src, dst_ref=dst, send_sem=send_sem, recv_sem=recv_sem,
            device_id={"dp": device}, device_id_type=MESH,
        )
        copy.start()
        sent.append(copy)
        return copy

    def rows_of(slot):
        if slot == chips:
            return half, pl.ds(row_half, rank - row_half)
        if slot == half:
            return half, pl.ds(0, row_half)
        return slot, pl.ds(0, rank)

    def ring(layer, src, slot, device):
        where, rows = rows_of(slot)
        return send(
            src.at[rows], held.at[layer, 0, where, rows],
            ring_send.at[layer, slot], ring_recv.at[layer, slot], device,
        )

    def across(layer, slot):
        where, rows = rows_of(slot)
        return send(
            held.at[layer, 0, where, rows], held.at[layer, 1, where, rows],
            pair_send.at[layer, slot], pair_recv.at[layer, slot], pair,
        )

    def arrived(layer, bank, slot):
        where, rows = rows_of(slot)
        ref = held.at[layer, bank, where, rows]
        sems = (pair_send, pair_recv) if bank else (ring_send, ring_recv)
        pltpu.make_async_remote_copy(
            src_ref=ref, dst_ref=ref, send_sem=sems[0].at[layer, slot], recv_sem=sems[1].at[layer, slot],
            device_id={"dp": pair}, device_id_type=MESH,
        ).wait_recv()

    for layer in range(layers):
        ring(layer, fac_ref.at[layer], 1, up)
        ring(layer, fac_ref.at[layer], chips - 1, down)
    load_own.wait()
    for layer in range(layers):
        across(layer, 0)

    load_grad.wait()
    load_pout.wait()
    count = len_ref[0]
    kept = (lax.broadcasted_iota(jnp.int32, (rank, LEN), 1) < count).astype(jnp.float32)
    left = []
    for layer in range(layers):
        turned[layer] = kept * lax.dot_general(
            pout[layer], grad[layer], ROWS_BY_ROWS, preferred_element_type=jnp.float32
        )
        left.append(jnp.concatenate(
            [turned[layer, pl.ds(0, rank // 2, stride=2), :], turned[layer, pl.ds(1, rank // 2, stride=2), :]],
            axis=0,
        ))

    totals = [jnp.zeros((LEN, rank), jnp.float32) for _ in range(layers)]

    def add(layer, bank, slot):
        owner = device_at(place - slot, core if bank == 0 else 1 - core)
        columns = pl.ds(pl.multiple_of(owner * depth, depth), depth)
        totals[layer] += lax.dot_general(
            hid[layer, :, columns], held[layer, bank, slot], ROWS_BY_ROWS, preferred_element_type=jnp.float32
        )

    def finish(layer):
        sketch = lax.dot_general(
            left[layer], totals[layer], (((1,), (0,)), ((), ())),
            precision=lax.Precision.HIGHEST, preferred_element_type=jnp.float32,
        ) * (1.0 / math.sqrt(LEN))
        flat = jnp.concatenate([sketch[: rank // 2], sketch[rank // 2 :]], axis=1)
        sketches[layer, me] = flat.astype(jnp.bfloat16)
        mine = sketches.at[layer, me]
        if layer in RELAYED:
            send(mine, mine, sk_send.at[layer, 1], sk_recv.at[layer, 1], pair)
        for step in range(2, n, 2) if layer in RELAYED else range(1, n):
            send(mine, mine, sk_send.at[layer, step], sk_recv.at[layer, step], lax.rem(me + step, n))

    for layer in range(layers):
        load_hid[layer].wait()
        add(layer, 0, 0)
    for hop in range(1, half + 1):
        for layer in range(layers):
            if hop < half:
                arrived(layer, 0, hop)
                ring(layer, held.at[layer, 0, hop], hop + 1, up)
                across(layer, hop)
                arrived(layer, 0, chips - hop)
                ring(layer, held.at[layer, 0, chips - hop], chips - hop - 1 if hop + 1 < half else chips, down)
                across(layer, chips - hop)
                add(layer, 0, hop)
                add(layer, 0, chips - hop)
            else:
                arrived(layer, 0, half)
                across(layer, half)
                arrived(layer, 0, chips)
                across(layer, chips)
                add(layer, 0, half)
            if hop == 1:
                arrived(layer, 1, 0)
                add(layer, 1, 0)
            else:
                for slot in (hop - 1, chips - hop + 1):
                    if hop < half or layer:
                        arrived(layer, 1, slot)
                        add(layer, 1, slot)
            if hop == half - 1 and layer == layers - 1:
                for early in range(layers - 1):
                    for slot in (hop, chips - hop):
                        arrived(early, 1, slot)
                        add(early, 1, slot)
            if hop == half:
                arrived(layer, 1, half)
                arrived(layer, 1, chips)
                add(layer, 1, half)
                finish(layer)

    def sketch_arrived(layer, step, source):
        ref = sketches.at[layer, lax.rem(source, n)]
        pltpu.make_async_remote_copy(
            src_ref=ref, dst_ref=ref, send_sem=sk_send.at[layer, step], recv_sem=sk_recv.at[layer, step],
            device_id={"dp": pair}, device_id_type=MESH,
        ).wait_recv()
        return ref

    for layer in RELAYED:
        for step in range(2, n, 2):
            ref = sketch_arrived(layer, step, me + n - step)
            send(ref, ref, sk_send.at[layer, step + 1], sk_recv.at[layer, step + 1], pair)

    last = len(sent) - (n - 1) - (n // 2 - 1)
    for copy in sent[:last]:
        copy.wait_send()
    load_query.wait()
    scores = jnp.zeros((query.shape[0], n), jnp.float32)
    width = rank * rank
    for layer in range(layers):
        if layer in RELAYED:
            for step in range(0, n, 2):
                sketch_arrived(layer, step + 1, pair + n - step)
        else:
            for step in range(1, n):
                sketch_arrived(layer, step, me + n - step)
        lines = width // 128
        spread[...] = sketches[layer].astype(jnp.float32).reshape(n * lines, 128)
        flat = jnp.concatenate(
            [spread[pl.ds(line, n, stride=lines), :].astype(jnp.bfloat16) for line in range(lines)], axis=1
        )
        scores += lax.dot_general(
            query[:, layer * width : (layer + 1) * width], flat, ROWS_BY_ROWS, preferred_element_type=jnp.float32
        )
    out_ref[...] = scores * (1.0 / math.sqrt(layers * width))
    for copy in sent[last:]:
        copy.wait_send()


def fused(n, hidden_in, out_grad, proj_hidden, proj_out, lengths, query_sketch):
    layers, tokens, hidden = hidden_in.shape
    depth, rank = proj_hidden.shape[1:]
    queries = query_sketch.shape[0]
    lines = rank * rank // 128
    slots = n // 2 + 1
    dma = pltpu.SemaphoreType.DMA
    return pl.pallas_call(
        functools.partial(fused_kernel, n),
        out_shape=jax.ShapeDtypeStruct((queries, n), jnp.float32),
        in_specs=[pl.BlockSpec(memory_space=pltpu.SMEM)] + [pl.BlockSpec(memory_space=pl.ANY)] * 5,
        out_specs=pl.BlockSpec(memory_space=pltpu.VMEM),
        scratch_shapes=[
            pltpu.VMEM((layers, tokens, hidden), jnp.bfloat16),
            pltpu.VMEM(out_grad.shape, jnp.bfloat16),
            pltpu.VMEM((layers, rank, proj_out.shape[1]), jnp.bfloat16),
            pltpu.VMEM(query_sketch.shape, jnp.bfloat16),
            pltpu.VMEM((layers, 2, n // 2, rank, depth), jnp.bfloat16),
            pltpu.VMEM((layers, rank, LEN), jnp.float32),
            pltpu.VMEM((layers, n, lines, 128), jnp.bfloat16),
            pltpu.VMEM((n * lines, 128), jnp.float32),
            dma((8,)),
            dma((layers, slots)),
            dma((layers, slots)),
            dma((layers, slots)),
            dma((layers, slots)),
            dma((layers, n)),
            dma((layers, n)),
        ],
        compiler_params=pltpu.CompilerParams(
            collective_id=0, has_side_effects=True, vmem_limit_bytes=63 << 20
        ),
        cost_estimate=pl.CostEstimate(
            flops=2 * layers * tokens * rank * (hidden + out_grad.shape[2]),
            bytes_accessed=2 * layers * tokens * (hidden + out_grad.shape[2]),
            transcendentals=0,
        ),
    )(
        lengths, hidden_in, out_grad, jnp.swapaxes(proj_hidden, 1, 2), jnp.swapaxes(proj_out, 1, 2), query_sketch
    )


def solution(mesh):
    n = mesh.shape["dp"]

    def on_device(hidden_in, out_grad, proj_hidden, proj_out, lengths, query_sketch):
        args = (hidden_in, out_grad, proj_hidden, proj_out, lengths, query_sketch)
        aligned = proj_hidden.shape[1] % 128 == 0 and proj_hidden.shape[2] == 64
        if aligned and lengths.shape[0] == 1 and out_grad.shape[1] == LEN and n % 4 == 0 and n >= 8:
            return fused(n, *args)
        return plain(*args)

    return jax.shard_map(
        on_device,
        mesh=mesh,
        in_specs=(
            P(None, ("groups", "dp"), None),
            P(None, ("groups", "dp"), None),
            P(None, "dp", None),
            P(),
            P(("groups", "dp")),
            P(("groups", "dp"), None),
        ),
        out_specs=P(("groups", "dp"), None),
        check_vma=False,
    )
```
